256 devices in a mesh: gx: 8 (over y, z_lo), gy: 32 (over x, z_hi, core).
Axes of the slice: x: 4, y: 4, z: 8 (z_hi: 4, z_lo: 2; z = z_hi * 2 + z_lo), core: 2. Of those that a mesh axis runs over, the one named last changes fastest.
Arguments:
- images: bfloat16 [196608, 1152], P(('gx', 'gy'))
- captions: bfloat16 [196608, 1152], P(('gx', 'gy'))
- logit_scale: float32 [1], replicated, may hold values from 10 to 120
Outputs:
- losses: float32 [196608], P(('gx', 'gy'))
- grad_images: float32 [196608, 1152], P(('gx', 'gy'))
- grad_captions: float32 [196608, 1152], P(('gx', 'gy'))
The draws below stay inside these ranges and needn't reach their ends.
All inputs are finite; a program needn't handle non-finite values.
Results may differ from the reference program's by a relative error of at most 0.0055.
The reference program's roundings to bfloat16 on the way count: a program that leaves them out, or rounds other values in their place, can miss the bound.
Values may be sent and summed in bfloat16 or wider, within the bound.
No kernel may reach another device: no remote copies, remote signals or barrier semaphores. Data moves between devices by JAX's collectives and lax.ppermute only.
A program may use at most 128 MiB of HBM per device.

```python
import jax
import jax.numpy as jnp
from jax import lax

WIDTH = 1152
BLOCK = 768
PAIRS = 196608


def pair_fields(key):
    key_a, key_b = jax.random.split(jax.random.fold_in(key, 11), 2)
    anchor = jax.random.normal(key_a, (PAIRS, WIDTH), jnp.float32)
    jitter = jax.random.normal(key_b, (PAIRS, WIDTH), jnp.float32)
    image_rows = anchor
    caption_rows = 0.6 * anchor + 0.8 * jitter
    return (image_rows, caption_rows)


def draw_images(key, part):
    image_rows, caption_rows = pair_fields(key)
    return image_rows.astype(jnp.bfloat16)


def draw_captions(key, part):
    image_rows, caption_rows = pair_fields(key)
    return caption_rows.astype(jnp.bfloat16)


def draw_logit_scale(key, part):
    return jnp.exp(jax.random.uniform(jax.random.fold_in(key, 23), (1,), jnp.float32, jnp.log(10.0), jnp.log(100.0)))


def setup_inputs(seed: int = 0) -> dict:
    streams_of = jax.random.split(jax.random.key(seed), 4)
    return {
        "images": draw_images(jax.random.fold_in(streams_of[3], 71), 0),
        "captions": draw_captions(jax.random.fold_in(streams_of[3], 71), 0),
        "logit_scale": draw_logit_scale(jax.random.fold_in(streams_of[3], 71), 0),
    }


def widen_unit(values):
    widened = values.astype(jnp.float32)
    inverse = lax.rsqrt(lax.optimization_barrier(jnp.sum(widened * widened, axis=-1, keepdims=True)) + 1e-06)
    return (widened * inverse, inverse)

def log_total(values, along):
    peak = lax.optimization_barrier(jnp.max(values, axis=along, keepdims=True))
    return jnp.squeeze(peak, along) + jnp.log(lax.optimization_barrier(jnp.sum(jnp.exp(values - peak), axis=along)))

def reference(images, captions, logit_scale):
    factor = logit_scale[0]
    img_unit, img_inverse = widen_unit(images)
    cap_unit, cap_inverse = widen_unit(captions)
    blocks = PAIRS // BLOCK
    img_blocks = img_unit.astype(jnp.bfloat16).reshape(blocks, BLOCK, WIDTH)
    cap_blocks = cap_unit.astype(jnp.bfloat16).reshape(blocks, BLOCK, WIDTH)
    indices = jnp.arange(blocks, dtype=jnp.int32)
    ones_block = jnp.eye(BLOCK, dtype=jnp.float32)
    zero_block = jnp.zeros((BLOCK, BLOCK), jnp.float32)

    def beside_all(stack, block):
        return jnp.concatenate([stack[(block - 1) % blocks], stack[block], stack[(block + 1) % blocks]], axis=0)

    def row_part(block):
        window = beside_all(cap_blocks, block)
        scores = factor * jnp.dot(img_blocks[block], window.T, preferred_element_type=jnp.float32)
        return (log_total(scores, 1), jnp.diagonal(scores[:, BLOCK:2 * BLOCK]))
    row_lse, positive = lax.map(row_part, indices)

    def col_part(block):
        window = beside_all(img_blocks, block)
        scores = factor * jnp.dot(window, cap_blocks[block].T, preferred_element_type=jnp.float32)
        return log_total(scores, 0)
    col_lse = lax.map(col_part, indices)

    def image_grad(block):
        window = beside_all(cap_blocks, block)
        scores = factor * jnp.dot(img_blocks[block], window.T, preferred_element_type=jnp.float32)
        columns = beside_all(col_lse, block)
        target = jnp.concatenate([zero_block, ones_block, zero_block], axis=1)
        weights = 0.5 * jnp.exp(scores - row_lse[block][:, None]) + 0.5 * jnp.exp(scores - columns[None, :]) - target
        return factor * jnp.dot(weights.astype(jnp.bfloat16), window, preferred_element_type=jnp.float32)

    def caption_grad(block):
        window = beside_all(img_blocks, block)
        scores = factor * jnp.dot(window, cap_blocks[block].T, preferred_element_type=jnp.float32)
        rows_lse = beside_all(row_lse, block)
        target = jnp.concatenate([zero_block, ones_block, zero_block], axis=0)
        weights = 0.5 * jnp.exp(scores - rows_lse[:, None]) + 0.5 * jnp.exp(scores - col_lse[block][None, :]) - target
        return factor * jnp.dot(weights.astype(jnp.bfloat16).T, window, preferred_element_type=jnp.float32)
    img_grad = lax.map(image_grad, indices).reshape(PAIRS, WIDTH)
    cap_grad = lax.map(caption_grad, indices).reshape(PAIRS, WIDTH)
    losses = (0.5 * (row_lse - positive) + 0.5 * (col_lse - positive)).reshape(PAIRS)
    grad_images = img_inverse * (img_grad - img_unit * lax.optimization_barrier(jnp.sum(img_unit * img_grad, axis=-1, keepdims=True)))
    grad_captions = cap_inverse * (cap_grad - cap_unit * lax.optimization_barrier(jnp.sum(cap_unit * cap_grad, axis=-1, keepdims=True)))
    return (losses, grad_images, grad_captions)
```

```python
import functools

import jax
import jax.numpy as jnp
from jax import lax
from jax.experimental import pallas as pl
from jax.experimental.pallas import tpu as pltpu
from jax.sharding import PartitionSpec as P

TILE = 256
LANES = 128
MIB = 1024 * 1024
F32, BF16 = jnp.float32, jnp.bfloat16
VMEM = pl.BlockSpec(memory_space=pltpu.VMEM)
SMEM = pl.BlockSpec(memory_space=pltpu.SMEM)
HBM = pl.BlockSpec(memory_space=pltpu.HBM)
PARTS = ((0, 256), (256, 256), (512, 256))


def array(dtype, *shape):
    return jax.ShapeDtypeStruct(shape, dtype)


def in_hbm(dtype, *shape):
    return pltpu.HBM(shape, dtype)


def call(kernel, ins, outs, shapes, name, macs=0, scratch=(), limit=6):
    def run(*operands):
        return inner(
            *(
                pltpu.with_memory_space_constraint(value, pltpu.HBM) if spec is HBM else value
                for value, spec in zip(operands, ins, strict=True)
            )
        )

    inner = pl.pallas_call(
        kernel,
        in_specs=ins,
        out_specs=outs,
        out_shape=shapes,
        scratch_shapes=list(scratch),
        compiler_params=pltpu.CompilerParams(vmem_limit_bytes=limit * MIB),
        cost_estimate=pl.CostEstimate(
            flops=2 * macs, bytes_accessed=2_000_000, transcendentals=0
        ),
        name=name,
    )
    return run


def tiles(height):
    return [slice(start, min(start + TILE, height)) for start in range(0, height, TILE)]


def dot_nt(a, b):
    return lax.dot_general(a, b, (((1,), (1,)), ((), ())), preferred_element_type=F32)


def to_lanes(column):
    return jnp.transpose(jnp.broadcast_to(column, (column.shape[0], LANES)))[0:1, :]


def to_rows(lanes, width):
    block = jnp.transpose(jnp.broadcast_to(lanes, (LANES, lanes.shape[1])))
    copies = -(-width // LANES)
    return jnp.concatenate([block] * copies, axis=1)[:, :width]


def unit_rows(raw):
    wide = raw.astype(F32)
    inverse = lax.rsqrt(jnp.sum(wide * wide, axis=-1, keepdims=True) + 1e-06)
    return wide * inverse, inverse


def diagonal(shape, start):
    here = lax.broadcasted_iota(jnp.int32, shape, 0) + start
    return here == lax.broadcasted_iota(jnp.int32, shape, 1)


def weigh(scores, own_lse, other_lse, start=None):
    weights = 0.5 * jnp.exp(scores - own_lse) + 0.5 * jnp.exp(scores - other_lse)
    if start is not None:
        weights = weights - diagonal(scores.shape, start).astype(F32)
    return weights.astype(BF16)


def project(raw, grad):
    unit, inverse = unit_rows(raw)
    return inverse * (grad - unit * jnp.sum(unit * grad, axis=-1, keepdims=True))


def normalize(*arrays):
    height, width = arrays[0].shape
    count = len(arrays)

    def kernel(*refs):
        for src, dst in zip(refs[:count], refs[count:]):
            for rows in tiles(height):
                dst[rows, :] = unit_rows(src[rows, :])[0].astype(BF16)

    return call(
        kernel, [VMEM] * count, [VMEM] * count, [array(BF16, height, width)] * count, "unit_rows"
    )(*arrays)


def start_copy(source, target, sem):
    copy = pltpu.make_async_copy(source, target, sem)
    copy.start()
    return copy


def start_copy(source, target, sem):
    copy = pltpu.make_async_copy(source, target, sem)
    copy.start()
    return copy


def near_scores(scale, img, cap, mate_img, mate_cap):
    height, width = img.shape

    def kernel(scale_ref, img_ref, cap_ref, mate_img_ref, mate_cap_ref, *outs):
        factor = scale_ref[0]
        for own_ref, opp_ref, mate_ref, (first_ref, second_ref, stats_ref) in (
            (img_ref, cap_ref, mate_cap_ref, outs[:3]),
            (cap_ref, img_ref, mate_img_ref, outs[3:]),
        ):
            for rows in tiles(height):
                first = factor * dot_nt(own_ref[rows, :], opp_ref[...])
                second = factor * dot_nt(own_ref[rows, :], mate_ref[...])
                first_ref[rows, :] = first
                second_ref[rows, :] = second
                peak = jnp.maximum(
                    jnp.max(first, axis=1, keepdims=True), jnp.max(second, axis=1, keepdims=True)
                )
                total = jnp.sum(jnp.exp(first - peak), axis=1, keepdims=True) + jnp.sum(
                    jnp.exp(second - peak), axis=1, keepdims=True
                )
                diag = jnp.where(diagonal(first.shape, rows.start), first, 0.0)
                stats_ref[0:1, rows] = to_lanes(peak)
                stats_ref[1:2, rows] = to_lanes(total)
                stats_ref[2:3, rows] = to_lanes(jnp.sum(diag, axis=1, keepdims=True))

    square, stats = array(F32, height, height), array(F32, 8, height)
    return call(
        kernel,
        [SMEM] + [VMEM] * 4,
        [VMEM] * 6,
        [square, square, stats] * 2,
        "near_scores",
        4 * height * height * width,
    )(scale, img, cap, mate_img, mate_cap)


def far_scores(scale, own, far, stats):
    height, width = own.shape

    def kernel(scale_ref, own_ref, far_ref, stats_ref, scores_ref, half_ref, msg_ref):
        factor = scale_ref[0]
        for rows in tiles(height):
            half_ref[rows, :] = unit_rows(far_ref[rows, :])[0].astype(BF16)
        tops, sums = [], []
        for rows in tiles(height):
            scores = factor * dot_nt(own_ref[rows, :], half_ref[...])
            scores_ref[rows, :] = scores
            peak = jnp.max(scores, axis=1, keepdims=True)
            total = jnp.sum(jnp.exp(scores - peak), axis=1, keepdims=True)
            peak, total = to_lanes(peak), to_lanes(total)
            before = stats_ref[0:1, rows]
            top = jnp.maximum(before, peak)
            summed = stats_ref[1:2, rows] * jnp.exp(before - top) + total * jnp.exp(peak - top)
            msg_ref[0:1, rows] = top + jnp.log(summed)
            tops.append(jnp.max(scores, axis=0, keepdims=True))
            sums.append(jnp.sum(jnp.exp(scores - tops[-1]), axis=0, keepdims=True))
        col_top = functools.reduce(jnp.maximum, tops)
        msg_ref[1:2, :] = col_top
        msg_ref[2:3, :] = sum(s * jnp.exp(t - col_top) for s, t in zip(sums, tops))

    return call(
        kernel,
        [SMEM] + [VMEM] * 3,
        [VMEM] * 3,
        [array(F32, height, height), array(BF16, height, width), array(F32, 8, height)],
        "far_scores",
        height * height * width,
    )(scale, own, far, stats)


def finish_columns(col_stats, far_message, message, row_stats):
    height = col_stats.shape[1]

    def kernel(stats_ref, far_ref, msg_ref, row_ref, out_ref, loss_ref):
        before, far_top = stats_ref[0:1, :], far_ref[1:2, :]
        top = jnp.maximum(before, far_top)
        summed = stats_ref[1:2, :] * jnp.exp(before - top) + far_ref[2:3, :] * jnp.exp(
            far_top - top
        )
        lse = top + jnp.log(summed)
        out_ref[0:1, :] = lse
        positive = row_ref[2:3, :]
        loss = 0.5 * (msg_ref[0:1, :] - positive) + 0.5 * (lse - positive)
        loss_ref[...] = loss.reshape(height)

    return call(
        kernel,
        [VMEM] * 4,
        [VMEM] * 2,
        [array(F32, 8, height), array(F32, height)],
        "finish_columns",
    )(col_stats, far_message, message, row_stats)


def caption_gradient(scale, scores, own, own_message, messages, others, part, far_message):
    height, width = own.shape
    count, (start, length) = len(others), PARTS[0]

    def kernel(scale_ref, own_ref, own_msg_ref, part_ref, far_msg_ref, *refs):
        score_refs, msg_refs, other_refs = (refs[i * count : (i + 1) * count] for i in range(3))
        factor = scale_ref[0]
        other = unit_rows(part_ref[...])[0].astype(BF16)
        for rows in tiles(height):
            weights = weigh(
                factor * dot_nt(own_ref[rows, :], other),
                to_rows(own_msg_ref[0:1, rows], length),
                far_msg_ref[0:1, start : start + length],
            )
            total = jnp.dot(weights, other, preferred_element_type=F32)
            own_lse = to_rows(own_msg_ref[0:1, rows], height)
            for k in range(count):
                weights = weigh(
                    score_refs[k][rows, :],
                    own_lse,
                    msg_refs[k][0:1, :],
                    rows.start if k == 0 else None,
                )
                total += jnp.dot(weights, other_refs[k][...], preferred_element_type=F32)
            refs[-1][rows, :] = total

    return call(
        kernel,
        [SMEM] + [VMEM] * (4 + 3 * count),
        VMEM,
        array(F32, height, width),
        "caption_gradient",
        count * height * height * width + 2 * length * height * width,
    )(scale, own, own_message, part, far_message, *scores, *messages, *others)


def image_gradient(scale, scores, own_message, messages, others, raw):
    height, width = raw.shape
    rows_of = tiles(height)
    count = len(others)

    def kernel(scale_ref, own_ref, *refs):
        score_refs, msg_refs, other_refs = (refs[i * count : (i + 1) * count] for i in range(3))
        raw_ref, out_ref, stage, sems = refs[3 * count :]
        factor = scale_ref[0]
        copies = []
        for index, rows in enumerate(rows_of):
            own_lse = to_rows(own_ref[0:1, rows], height)
            total = None
            for k in range(count):
                weights = weigh(
                    score_refs[k][rows, :],
                    own_lse,
                    msg_refs[k][0:1, :],
                    rows.start if k == 0 else None,
                )
                term = jnp.dot(weights, other_refs[k][...], preferred_element_type=F32)
                total = term if total is None else total + term
            stage[rows, :] = project(raw_ref[rows, :], factor * total)
            copies.append(start_copy(stage.at[rows, :], out_ref.at[rows, :], sems.at[index]))
        for copy in copies:
            copy.wait()

    return call(
        kernel,
        [SMEM] + [VMEM] * (2 + 3 * count),
        HBM,
        in_hbm(F32, height, width),
        "image_gradient",
        count * height * height * width,
        [pltpu.VMEM((height, width), F32), pltpu.SemaphoreType.DMA((len(rows_of),))],
        limit=12,
    )(scale, own_message, *scores, *messages, *others, raw)


def part_gradient(scale, own, own_message, part, message, start, total, raw=None):
    height, width = own.shape
    rows_of = tiles(height)
    count = part.shape[0]
    final = raw is not None

    def kernel(scale_ref, own_ref, own_msg_ref, part_ref, msg_ref, total_ref, *refs):
        factor = scale_ref[0]
        copies = []
        other = unit_rows(part_ref[...])[0].astype(BF16)
        for index, rows in enumerate(rows_of):
            weights = weigh(
                factor * dot_nt(own_ref[rows, :], other),
                to_rows(own_msg_ref[0:1, rows], count),
                msg_ref[0:1, start : start + count],
            )
            total = total_ref[rows, :] + jnp.dot(weights, other, preferred_element_type=F32)
            if final:
                raw_ref, out_ref, stage, sems = refs
                stage[rows, :] = project(raw_ref[rows, :], factor * total)
                copies.append(start_copy(stage.at[rows, :], out_ref.at[rows, :], sems.at[index]))
            else:
                refs[0][rows, :] = total
        for copy in copies:
            copy.wait()

    return call(
        kernel,
        [SMEM] + [VMEM] * (6 if final else 5),
        HBM if final else VMEM,
        (in_hbm if final else array)(F32, height, width),
        "last_part_gradient" if final else "part_gradient",
        2 * count * height * width,
        [pltpu.VMEM((height, width), F32), pltpu.SemaphoreType.DMA((len(rows_of),))]
        if final
        else [],
        limit=12 if final else 6,
    )(scale, own, own_message, part, message, total, *([raw] if final else []))


def body(mate_pairs, far_pairs, images, captions, logit_scale):
    axes = ("gx", "gy")
    to_mate = functools.partial(lax.ppermute, axis_name=axes, perm=mate_pairs)
    to_far = functools.partial(lax.ppermute, axis_name=axes, perm=far_pairs)

    def after(value, cause):
        return lax.optimization_barrier((value, cause))[0]

    def part_of(index):
        start, count = PARTS[index]
        return lax.slice_in_dim(images, start, start + count, axis=0)

    far_raw = to_far(captions)
    parts = [to_far(part_of(0))]
    mate_raw = (to_mate(images), to_mate(captions))

    img, cap = normalize(images, captions)
    mate_img, mate_cap = normalize(*mate_raw)
    img_cap, img_mate, row_stats, cap_img, cap_mate, col_stats = near_scores(
        logit_scale, img, cap, mate_img, mate_cap
    )
    img_far, far_cap, message = far_scores(logit_scale, img, far_raw, row_stats)
    far_message = to_far(message)
    mate_message = to_mate(message)
    parts.append(to_far(after(part_of(1), message)))

    col_message, losses = finish_columns(col_stats, far_message, message, row_stats)
    far_col = to_far(col_message)
    mate_col = to_mate(col_message)
    for index in range(2, len(PARTS)):
        parts.append(to_far(after(part_of(index), col_message)))

    total = caption_gradient(
        logit_scale,
        (cap_img, cap_mate),
        cap,
        col_message,
        (message, mate_message),
        (img, mate_img),
        parts[0],
        far_message,
    )
    grad_images = image_gradient(
        logit_scale,
        (img_cap, img_mate, img_far),
        message,
        (col_message, mate_col, far_col),
        (cap, mate_cap, far_cap),
        images,
    )
    total, grad_images = lax.optimization_barrier((total, grad_images))
    for index, part in enumerate(parts):
        if index == 0:
            continue
        total = part_gradient(
            logit_scale,
            cap,
            col_message,
            part,
            far_message,
            PARTS[index][0],
            total,
            captions if index == len(parts) - 1 else None,
        )
    return losses, grad_images, total


def solution(mesh):
    devices = mesh.size
    mate_pairs = [(i, i ^ 1) for i in range(devices)]
    far_pairs = [(i, (i + 2 * (i % 2) - 1) % devices) for i in range(devices)]
    return jax.shard_map(
        functools.partial(body, mate_pairs, far_pairs),
        mesh=mesh,
        in_specs=(P(("gx", "gy"), None), P(("gx", "gy"), None), P()),
        out_specs=(P(("gx", "gy")), P(("gx", "gy"), None), P(("gx", "gy"), None)),
        check_vma=False,
    )
```

```python
import functools

import jax
import jax.numpy as jnp
from jax import lax
from jax.experimental import pallas as pl
from jax.experimental.pallas import tpu as pltpu
from jax.sharding import PartitionSpec as P

TILE = 256
LANES = 128
MIB = 1024 * 1024
F32, BF16 = jnp.float32, jnp.bfloat16
VMEM = pl.BlockSpec(memory_space=pltpu.VMEM)
SMEM = pl.BlockSpec(memory_space=pltpu.SMEM)
HBM = pl.BlockSpec(memory_space=pltpu.HBM)
PARTS = ((0, 320), (320, 256), (576, 192))


def array(dtype, *shape):
    return jax.ShapeDtypeStruct(shape, dtype)


def in_hbm(dtype, *shape):
    return pltpu.HBM(shape, dtype)


def call(kernel, ins, outs, shapes, name, macs=0, scratch=(), limit=6):
    def run(*operands):
        return inner(
            *(
                pltpu.with_memory_space_constraint(value, pltpu.HBM) if spec is HBM else value
                for value, spec in zip(operands, ins, strict=True)
            )
        )

    inner = pl.pallas_call(
        kernel,
        in_specs=ins,
        out_specs=outs,
        out_shape=shapes,
        scratch_shapes=list(scratch),
        compiler_params=pltpu.CompilerParams(vmem_limit_bytes=limit * MIB),
        cost_estimate=pl.CostEstimate(
            flops=2 * macs, bytes_accessed=2_000_000, transcendentals=0
        ),
        name=name,
    )
    return run


def tiles(height):
    return [slice(start, min(start + TILE, height)) for start in range(0, height, TILE)]


def dot_nt(a, b):
    return lax.dot_general(a, b, (((1,), (1,)), ((), ())), preferred_element_type=F32)


def to_lanes(column):
    return jnp.transpose(jnp.broadcast_to(column, (column.shape[0], LANES)))[0:1, :]


def to_rows(lanes, width):
    block = jnp.transpose(jnp.broadcast_to(lanes, (LANES, lanes.shape[1])))
    copies = -(-width // LANES)
    return jnp.concatenate([block] * copies, axis=1)[:, :width]


def unit_rows(raw):
    wide = raw.astype(F32)
    inverse = lax.rsqrt(jnp.sum(wide * wide, axis=-1, keepdims=True) + 1e-06)
    return wide * inverse, inverse


def joint_lse(peak, total, other_peak, other_total):
    top = jnp.maximum(peak, other_peak)
    return top + jnp.log(total * jnp.exp(peak - top) + other_total * jnp.exp(other_peak - top))


def diagonal(shape, start):
    here = lax.broadcasted_iota(jnp.int32, shape, 0) + start
    return here == lax.broadcasted_iota(jnp.int32, shape, 1)


def weigh(scores, own_lse, other_lse, start=None):
    weights = 0.5 * jnp.exp(scores - own_lse) + 0.5 * jnp.exp(scores - other_lse)
    if start is not None:
        weights = weights - diagonal(scores.shape, start).astype(F32)
    return weights.astype(BF16)


def project(raw, grad):
    unit, inverse = unit_rows(raw)
    return inverse * (grad - unit * jnp.sum(unit * grad, axis=-1, keepdims=True))


def normalize(*arrays):
    height, width = arrays[0].shape
    count = len(arrays)

    def kernel(*refs):
        for src, dst in zip(refs[:count], refs[count:]):
            for rows in tiles(height):
                dst[rows, :] = unit_rows(src[rows, :])[0].astype(BF16)

    return call(
        kernel, [VMEM] * count, [VMEM] * count, [array(BF16, height, width)] * count, "unit_rows"
    )(*arrays)


def start_copy(source, target, sem):
    copy = pltpu.make_async_copy(source, target, sem)
    copy.start()
    return copy


def start_copy(source, target, sem):
    copy = pltpu.make_async_copy(source, target, sem)
    copy.start()
    return copy


def near_scores(scale, img, cap, mate_img, mate_cap):
    height, width = img.shape

    def kernel(scale_ref, img_ref, cap_ref, mate_img_ref, mate_cap_ref, *outs):
        factor = scale_ref[0]
        for own_ref, opp_ref, mate_ref, (first_ref, second_ref, stats_ref) in (
            (img_ref, cap_ref, mate_cap_ref, outs[:3]),
            (cap_ref, img_ref, mate_img_ref, outs[3:]),
        ):
            for rows in tiles(height):
                first = factor * dot_nt(own_ref[rows, :], opp_ref[...])
                second = factor * dot_nt(own_ref[rows, :], mate_ref[...])
                first_ref[rows, :] = first
                second_ref[rows, :] = second
                peak = jnp.maximum(
                    jnp.max(first, axis=1, keepdims=True), jnp.max(second, axis=1, keepdims=True)
                )
                total = jnp.sum(jnp.exp(first - peak), axis=1, keepdims=True) + jnp.sum(
                    jnp.exp(second - peak), axis=1, keepdims=True
                )
                diag = jnp.where(diagonal(first.shape, rows.start), first, 0.0)
                stats_ref[0:1, rows] = to_lanes(peak)
                stats_ref[1:2, rows] = to_lanes(total)
                stats_ref[2:3, rows] = to_lanes(jnp.sum(diag, axis=1, keepdims=True))

    square, stats = array(F32, height, height), array(F32, 8, height)
    return call(
        kernel,
        [SMEM] + [VMEM] * 4,
        [VMEM] * 6,
        [square, square, stats] * 2,
        "near_scores",
        4 * height * height * width,
    )(scale, img, cap, mate_img, mate_cap)


def far_scores(scale, own, far, stats, col_stats):
    height, width = own.shape

    def kernel(
        scale_ref, own_ref, far_ref, stats_ref, col_stats_ref, scores_ref, half_ref, msg_ref
    ):
        factor = scale_ref[0]
        for rows in tiles(height):
            half_ref[rows, :] = unit_rows(far_ref[rows, :])[0].astype(BF16)
        tops, sums = [], []
        for rows in tiles(height):
            scores = factor * dot_nt(own_ref[rows, :], half_ref[...])
            scores_ref[rows, :] = scores
            peak = jnp.max(scores, axis=1, keepdims=True)
            total = jnp.sum(jnp.exp(scores - peak), axis=1, keepdims=True)
            peak, total = to_lanes(peak), to_lanes(total)
            msg_ref[0:1, rows] = joint_lse(
                stats_ref[0:1, rows], stats_ref[1:2, rows], peak, total
            )
            tops.append(jnp.max(scores, axis=0, keepdims=True))
            sums.append(jnp.sum(jnp.exp(scores - tops[-1]), axis=0, keepdims=True))
        col_top = functools.reduce(jnp.maximum, tops)
        col_sum = sum(s * jnp.exp(t - col_top) for s, t in zip(sums, tops))
        msg_ref[1:2, :] = col_top
        msg_ref[2:3, :] = col_sum
        msg_ref[3:5, :] = col_stats_ref[0:2, :]

    return call(
        kernel,
        [SMEM] + [VMEM] * 4,
        [VMEM] * 3,
        [array(F32, height, height), array(BF16, height, width), array(F32, 8, height)],
        "far_scores",
        height * height * width,
    )(scale, own, far, stats, col_stats)


def finish_columns(far_message, message, row_stats):
    height = message.shape[1]

    def kernel(far_ref, msg_ref, row_ref, out_ref, loss_ref):
        def column_lse(near, far):
            return joint_lse(near[3:4, :], near[4:5, :], far[1:2, :], far[2:3, :])

        lse = column_lse(msg_ref, far_ref)
        out_ref[0:1, :] = lse
        out_ref[1:2, :] = column_lse(far_ref, msg_ref)
        positive = row_ref[2:3, :]
        loss = 0.5 * (msg_ref[0:1, :] - positive) + 0.5 * (lse - positive)
        loss_ref[...] = loss.reshape(height)

    return call(
        kernel,
        [VMEM] * 3,
        [VMEM] * 2,
        [array(F32, 8, height), array(F32, height)],
        "finish_columns",
    )(far_message, message, row_stats)


def caption_gradient(scale, scores, own, own_message, messages, others, part, far_message):
    height, width = own.shape
    count, (start, length) = len(others), PARTS[0]

    def kernel(scale_ref, own_ref, own_msg_ref, part_ref, far_msg_ref, *refs):
        score_refs, msg_refs, other_refs = (refs[i * count : (i + 1) * count] for i in range(3))
        factor = scale_ref[0]
        other = unit_rows(part_ref[...])[0].astype(BF16)
        for rows in tiles(height):
            weights = weigh(
                factor * dot_nt(own_ref[rows, :], other),
                to_rows(own_msg_ref[0:1, rows], length),
                far_msg_ref[0:1, start : start + length],
            )
            total = jnp.dot(weights, other, preferred_element_type=F32)
            own_lse = to_rows(own_msg_ref[0:1, rows], height)
            for k in range(count):
                weights = weigh(
                    score_refs[k][rows, :],
                    own_lse,
                    msg_refs[k][0:1, :],
                    rows.start if k == 0 else None,
                )
                total += jnp.dot(weights, other_refs[k][...], preferred_element_type=F32)
            refs[-1][rows, :] = total

    return call(
        kernel,
        [SMEM] + [VMEM] * (4 + 3 * count),
        VMEM,
        array(F32, height, width),
        "caption_gradient",
        count * height * height * width + 2 * length * height * width,
    )(scale, own, own_message, part, far_message, *scores, *messages, *others)


def image_gradient(scale, scores, own_message, messages, others, raw):
    height, width = raw.shape
    rows_of = tiles(height)
    count = len(others)
    messages, lse_rows = zip(*messages)

    def kernel(scale_ref, own_ref, raw_ref, *refs):
        score_refs, msg_refs, other_refs = (refs[i * count : (i + 1) * count] for i in range(3))
        out_ref, stage, sems = refs[3 * count :]
        factor = scale_ref[0]
        copies = []
        for index, rows in enumerate(rows_of):
            own_lse = to_rows(own_ref[0:1, rows], height)
            total = None
            for k in range(count):
                weights = weigh(
                    score_refs[k][rows, :],
                    own_lse,
                    msg_refs[k][lse_rows[k] : lse_rows[k] + 1, :],
                    rows.start if k == 0 else None,
                )
                term = jnp.dot(weights, other_refs[k][...], preferred_element_type=F32)
                total = term if total is None else total + term
            stage[rows, :] = project(raw_ref[rows, :], factor * total)
            copies.append(start_copy(stage.at[rows, :], out_ref.at[rows, :], sems.at[index]))
        for copy in copies:
            copy.wait()

    return call(
        kernel,
        [SMEM] + [VMEM] * (2 + 3 * count),
        HBM,
        in_hbm(F32, height, width),
        "image_gradient",
        count * height * height * width,
        [pltpu.VMEM((height, width), F32), pltpu.SemaphoreType.DMA((len(rows_of),))],
        limit=12,
    )(scale, own_message, raw, *scores, *messages, *others)


def part_gradient(scale, own, own_message, part, message, start, total, raw=None):
    height, width = own.shape
    rows_of = tiles(height)
    count = part.shape[0]
    final = raw is not None

    def kernel(scale_ref, own_ref, own_msg_ref, part_ref, msg_ref, total_ref, *refs):
        factor = scale_ref[0]
        copies = []
        other = unit_rows(part_ref[...])[0].astype(BF16)
        for index, rows in enumerate(rows_of):
            weights = weigh(
                factor * dot_nt(own_ref[rows, :], other),
                to_rows(own_msg_ref[0:1, rows], count),
                msg_ref[0:1, start : start + count],
            )
            total = total_ref[rows, :] + jnp.dot(weights, other, preferred_element_type=F32)
            if final:
                raw_ref, out_ref, stage, sems = refs
                stage[rows, :] = project(raw_ref[rows, :], factor * total)
                copies.append(start_copy(stage.at[rows, :], out_ref.at[rows, :], sems.at[index]))
            else:
                refs[0][rows, :] = total
        for copy in copies:
            copy.wait()

    return call(
        kernel,
        [SMEM] + [VMEM] * (6 if final else 5),
        HBM if final else VMEM,
        (in_hbm if final else array)(F32, height, width),
        "last_part_gradient" if final else "part_gradient",
        2 * count * height * width,
        [pltpu.VMEM((height, width), F32), pltpu.SemaphoreType.DMA((len(rows_of),))]
        if final
        else [],
        limit=12 if final else 6,
    )(scale, own, own_message, part, message, total, *([raw] if final else []))


def body(mate_pairs, far_pairs, images, captions, logit_scale):
    axes = ("gx", "gy")
    to_mate = functools.partial(lax.ppermute, axis_name=axes, perm=mate_pairs)
    to_far = functools.partial(lax.ppermute, axis_name=axes, perm=far_pairs)

    def after(value, cause):
        return lax.optimization_barrier((value, cause))[0]

    def part_of(index):
        start, count = PARTS[index]
        return lax.slice_in_dim(images, start, start + count, axis=0)

    far_raw = to_far(captions)
    parts = [to_far(part_of(0))]
    mate_raw = (to_mate(images), to_mate(captions))

    img, cap = normalize(images, captions)
    mate_img, mate_cap = normalize(*mate_raw)
    img_cap, img_mate, row_stats, cap_img, cap_mate, col_stats = near_scores(
        logit_scale, img, cap, mate_img, mate_cap
    )

    img_far, far_cap, message = far_scores(logit_scale, img, far_raw, row_stats, col_stats)
    far_message = to_far(message)
    mate_message = to_mate(message)
    for index in range(1, len(PARTS)):
        parts.append(to_far(after(part_of(index), message)))

    col_message, losses = finish_columns(far_message, message, row_stats)
    mate_col = to_mate(col_message)

    total = caption_gradient(
        logit_scale,
        (cap_img, cap_mate),
        cap,
        col_message,
        (message, mate_message),
        (img, mate_img),
        parts[0],
        far_message,
    )
    mate_col, total = lax.optimization_barrier((mate_col, total))
    grad_images = image_gradient(
        logit_scale,
        (img_cap, img_far, img_mate),
        message,
        ((col_message, 0), (col_message, 1), (mate_col, 0)),
        (cap, far_cap, mate_cap),
        images,
    )
    total, grad_images = lax.optimization_barrier((total, grad_images))
    for index in range(1, len(PARTS)):
        total = part_gradient(
            logit_scale,
            cap,
            col_message,
            parts[index],
            far_message,
            PARTS[index][0],
            total,
            captions if index == len(PARTS) - 1 else None,
        )
    return losses, grad_images, total


def solution(mesh):
    devices = mesh.size
    mate_pairs = [(i, i ^ 1) for i in range(devices)]
    far_pairs = [(i, (i + 2 * (i % 2) - 1) % devices) for i in range(devices)]
    return jax.shard_map(
        functools.partial(body, mate_pairs, far_pairs),
        mesh=mesh,
        in_specs=(P(("gx", "gy"), None), P(("gx", "gy"), None), P()),
        out_specs=(P(("gx", "gy")), P(("gx", "gy"), None), P(("gx", "gy"), None)),
        check_vma=False,
    )
```
